128 devices in a mesh: prow: 32 (over y, z, core), pcol: 4 (over x).
Axes of the slice: x: 4, y: 4, z: 4, core: 2. Of those that a mesh axis runs over, the one named last changes fastest.
Arguments:
- matrix: float32 [24576, 16384], P('prow', 'pcol'), may hold values from -6 to 6
- lower_panels: float32 [2, 24576, 256], P(None, ('prow', 'pcol')), may hold values from -0.375 to 0.375
- inverses: float32 [2, 256, 256], replicated
- pivots: int32 [2, 256], replicated, may hold values from 256 to 24575, as said below
Outputs:
- updated: float32 [24576, 16384], P('prow', 'pcol')
The draws below stay inside these ranges and needn't reach their ends.
Inputs may be any that keep to these rules, and one draw needn't show every extreme that they name: `pivots`: the 256 entries of panel k are distinct matrix rows, each at least (k + 1) * 256; among them is a row of matrix block k + 1 and a row of matrix block k + 32 // 2; their spread over process rows is uneven.
All inputs are finite; a program needn't handle non-finite values.
Results may differ from the reference program's by a relative error of at most 0.0001.
Values sent between devices are 32-bit elements; how exact they have to be, the bound alone decides.
No kernel may reach another device: no remote copies, remote signals or barrier semaphores. Data moves between devices by JAX's collectives and lax.ppermute only.
A program may use at most 128 MiB of HBM per device.

```python
import math
import jax
import jax.numpy as jnp
from jax import lax

NB = 256
ROW_DEV = 768
NR = 24576
NC = 16384
N_PROW = 32


def draw_inverses(key, part):
    key = jax.random.fold_in(key, 11)
    row_pos = jnp.arange(NB)[:, None]
    col_pos = jnp.arange(NB)[None, :]
    entries = jax.random.normal(key, (2, NB, NB), jnp.float32) / math.sqrt(NB)
    return jnp.where(col_pos < row_pos, entries, jnp.where(col_pos == row_pos, 1.0, 0.0)).astype(jnp.float32)


def draw_pivots(key, part):
    key = jax.random.fold_in(key, 7)
    prow_count = NR // ROW_DEV
    row_ids = jnp.arange(NR, dtype=jnp.int32)
    owner_rank = row_ids // NB % prow_count
    chosen_all = []
    for panel in range(2):
        panel_key = jax.random.fold_in(key, panel)
        key_prefer, key_jitter, key_forced = jax.random.split(panel_key, 3)
        prefer = jax.random.randint(key_prefer, (prow_count,), 0, 4096)
        jitter = jax.random.randint(key_jitter, (NR,), 0, 4096)
        offsets = jax.random.randint(key_forced, (2,), 0, NB)
        near_row = (panel + 1) * NB + offsets[0]
        far_row = (panel + prow_count // 2) * NB + offsets[1]
        scores = jnp.where(row_ids >= (panel + 1) * NB, prefer[owner_rank] + jitter, -1)
        forced = (row_ids == near_row) | (row_ids == far_row)
        scores = jnp.where(forced, 8192, scores)
        unique_scores = scores * NR + row_ids
        _, chosen = lax.top_k(unique_scores, NB)
        chosen_all.append(chosen.astype(jnp.int32))
    return jnp.stack(chosen_all).astype(jnp.int32)


def shard_levels(rng, dims, cuts, smallest, top_value):
    def one(dim, blocks):
        draws = jax.random.uniform(jax.random.fold_in(jax.random.fold_in(rng, 6), dim), (blocks,), jnp.float32, smallest / len(cuts), top_value / len(cuts))
        return jnp.repeat(jnp.exp(draws), dims[dim] // blocks).reshape((-1,) + (1,) * (len(dims) - dim - 1))

    loudness = one(*cuts[0])
    for cut in cuts[1:]:
        loudness = loudness * one(*cut)
    return loudness


def normal_values(key, dims, scale, reach, shards=(), kind=jnp.bfloat16):
    values = scale * jax.random.normal(key, dims, jnp.float32)
    if shards:
        values = values * shard_levels(key, dims, shards, -0.22, 0.18)
    return jnp.clip(values, -reach, reach).astype(kind)


def setup_inputs(seed: int = 0) -> dict:
    streams_of = jax.random.split(jax.random.key(seed), 5)
    return {
        "matrix": normal_values(streams_of[0], (NR, NC), 1.0, 6.0, ((0, 32), (1, 4)), jnp.float32),
        "lower_panels": normal_values(streams_of[1], (2, NR, NB), NB ** -0.5, 0.375, ((1, 128),), jnp.float32),
        "inverses": draw_inverses(jax.random.fold_in(streams_of[4], 71), 0),
        "pivots": draw_pivots(jax.random.fold_in(streams_of[4], 71), 0),
    }


def storage_row(matrix_row):
    blocks = matrix_row // NB
    return ((blocks % N_PROW) * ROW_DEV + (blocks // N_PROW) * NB + matrix_row % NB).astype(jnp.int32)


def reference(matrix, lower_panels, inverses, pivots):
    row_ids = jnp.arange(NR, dtype=jnp.int32)
    owner_rank = row_ids // ROW_DEV
    local_row = row_ids % ROW_DEV
    mat_index = ((local_row // NB) * N_PROW + owner_rank) * NB + local_row % NB
    updated = matrix
    for panel in range(2):
        top_start = panel * NB
        source = storage_row(pivots[panel])
        top_rows = storage_row(top_start + jnp.arange(NB, dtype=jnp.int32))
        raw_rows = updated[source]
        old_top = updated[top_rows]
        updated = updated.at[source].set(old_top)
        upper_rows = jnp.dot(inverses[panel], raw_rows, precision=lax.Precision.HIGHEST)
        updated = updated.at[top_rows].set(upper_rows)
        product = jnp.dot(lower_panels[panel], upper_rows, precision=lax.Precision.HIGHEST)
        updated = jnp.where((mat_index >= top_start + NB)[:, None], updated - product, updated)
    return updated
```

```python
import jax
import jax.numpy as jnp
from jax import lax
from jax.experimental import pallas as pl
from jax.experimental.pallas import tpu as pltpu
from jax.sharding import PartitionSpec as P

F32 = jnp.float32
BF16 = jnp.bfloat16
HIGHEST = lax.Precision.HIGHEST
NB = 256
LANES = 128
VMEM_LIMIT = 56 * 1024 * 1024


def rank_of(y, z, core):
    return ((y % 4) * 4 + z % 4) * 2 + core


def shift_pairs(dy, dz):
    return [
        (rank_of(y, z, core), rank_of(y + dy, z + dz, core))
        for y in range(4)
        for z in range(4)
        for core in range(2)
    ]


SWAP_CORES = [(rank, rank ^ 1) for rank in range(32)]


def shift(value, dy=0, dz=0):
    return lax.ppermute(value, "prow", shift_pairs(dy, dz))


def split_two(value):
    high = value.astype(BF16)
    low = (value - high.astype(F32)).astype(BF16)
    return high, low


def pick_kernel(place_ref, select_ref, matrix_ref, first_ref, second_ref):
    high, low = split_two(matrix_ref[...])
    select = select_ref[...]
    rows = jnp.dot(select, high, preferred_element_type=F32)
    rows = rows + jnp.dot(select, low, preferred_element_type=F32)
    for z_share in range(4):
        apart = (z_share + 4 - place_ref[2]) % 4
        part = rows[:, z_share * LANES : (z_share + 1) * LANES]
        first_ref[apart, 0] = part[:NB]
        second_ref[0, apart] = part[NB:]


def pick_rows(place, select, matrix):
    return pl.pallas_call(
        pick_kernel,
        out_shape=(
            jax.ShapeDtypeStruct((4, 4, NB, LANES), F32),
            jax.ShapeDtypeStruct((4, 4, NB, LANES), F32),
        ),
        grid_spec=pltpu.PrefetchScalarGridSpec(
            num_scalar_prefetch=1,
            grid=(4,),
            in_specs=[
                pl.BlockSpec(select.shape, lambda i, place: (0, 0)),
                pl.BlockSpec(
                    (matrix.shape[0], 4 * LANES),
                    lambda i, place: (0, place[0] * 4 + (place[1] + i) % 4),
                ),
            ],
            out_specs=(
                pl.BlockSpec((4, 1, NB, LANES), lambda i, place: (0, i, 0, 0)),
                pl.BlockSpec((1, 4, NB, LANES), lambda i, place: (i, 0, 0, 0)),
            ),
        ),
        compiler_params=pltpu.CompilerParams(vmem_limit_bytes=VMEM_LIMIT),
        cost_estimate=pl.CostEstimate(
            flops=2 * 2 * 512 * 768 * 2048, bytes_accessed=10 << 20, transcendentals=0
        ),
        name="pick_rows",
    )(place, select, matrix)


def top_parts_kernel(matrix_ref, *refs):
    outs, sems = refs[:8], refs[8]
    copies = []
    for core in range(2):
        for y in range(4):
            for z in range(4):
                columns = pl.ds((core * 16 + y * 4 + z) * LANES, LANES)
                copies.append((matrix_ref.at[pl.ds(0, 128), columns], outs[z].at[y, core]))
                copies.append((matrix_ref.at[pl.ds(128, 128), columns], outs[4 + y].at[z, core]))
    copies = [
        pltpu.make_async_copy(source, target, sems.at[i])
        for i, (source, target) in enumerate(copies)
    ]
    for copy in copies:
        copy.start()
    for copy in copies:
        copy.wait()


def top_parts(matrix):
    return pl.pallas_call(
        top_parts_kernel,
        out_shape=tuple(jax.ShapeDtypeStruct((4, 2, 128, LANES), F32) for _ in range(8)),
        in_specs=[pl.BlockSpec(memory_space=pl.ANY)],
        out_specs=tuple(pl.BlockSpec(memory_space=pl.ANY) for _ in range(8)),
        scratch_shapes=[pltpu.SemaphoreType.DMA((64,))],
        cost_estimate=pl.CostEstimate(flops=0, bytes_accessed=8 << 20, transcendentals=0),
        name="top_parts",
    )(matrix)


def scatter_tops(matrix, y, z):
    parts = top_parts(matrix)
    at_root = (y == 0) & (z == 0)

    def send(value, target_y, target_z, source_y, source_z):
        pairs = [
            (rank_of(sy, sz, core), rank_of(ty, tz, core))
            for sy, sz, ty, tz in zip(source_y, source_z, target_y, target_z)
            for core in range(2)
        ]
        return lax.ppermute(value, "prow", pairs)

    got_a = [send(parts[d], [0], [d], [0], [0]) for d in (1, 3, 2)]
    got_b = [send(parts[4 + d], [d], [0], [0], [0]) for d in (1, 3, 2)]
    held_a = jnp.where(at_root, parts[0], got_a[0] + got_a[1] + got_a[2])
    held_b = jnp.where(at_root, parts[4], got_b[0] + got_b[1] + got_b[2])
    four = list(range(4))
    got_a = [send(held_a[d], [d] * 4, four, [0] * 4, four) for d in (1, 3, 2)]
    got_b = [send(held_b[d], four, [d] * 4, four, [0] * 4) for d in (1, 3, 2)]
    share_a = jnp.where(y == 0, held_a[0], got_a[0] + got_a[1] + got_a[2])
    share_b = jnp.where(z == 0, held_b[0], got_b[0] + got_b[1] + got_b[2])
    return jnp.concatenate([share_a, share_b], axis=1)


def solve_kernel(raw0_ref, raw1_ref, inverse_ref, lower_ref, out_ref):
    def dot(a, b):
        return jnp.dot(a, b, precision=HIGHEST, preferred_element_type=F32)

    upper0 = dot(inverse_ref[0], raw0_ref[...])
    raw1 = raw1_ref[...] - dot(lower_ref[...], upper0)
    out_ref[:NB] = upper0
    out_ref[NB:] = dot(inverse_ref[1], raw1)


def solve(raw0, raw1, inverses, lower):
    return pl.pallas_call(
        solve_kernel,
        out_shape=jax.ShapeDtypeStruct((2 * NB, LANES), F32),
        cost_estimate=pl.CostEstimate(
            flops=6 * 3 * 2 * 256 * 256 * 128, bytes_accessed=1 << 20, transcendentals=0
        ),
        name="solve",
    )(raw0, raw1, inverses, lower)


def update_kernel(rank_ref, left_ref, keep_ref, matrix_ref, upper_ref, top_ref, out_ref):
    upper = jnp.concatenate([upper_ref[0, 0], upper_ref[1, 0]], axis=1)
    tops = jnp.concatenate(
        [
            jnp.concatenate([top_ref[0, core, 0], top_ref[1, core, 0]], axis=1)
            for core in range(2)
        ],
        axis=0,
    )
    upper_high, upper_low = split_two(upper)
    top_high, top_low = split_two(tops)
    right = jnp.concatenate([upper_high, upper_low, upper_high, top_high, top_low], axis=0)
    total = jnp.dot(left_ref[...], right, preferred_element_type=F32)
    out_ref[...] = matrix_ref[...] * keep_ref[...] + total

    @pl.when(rank_ref[0] == 0)
    def _():
        out_ref[:NB] = upper[:NB]

    @pl.when(rank_ref[0] == 1)
    def _():
        out_ref[:NB] = upper[NB:]


def update(rank, left, keep, matrix, upper, tops):
    rows, columns = matrix.shape
    width = 2 * LANES
    return pl.pallas_call(
        update_kernel,
        out_shape=jax.ShapeDtypeStruct(matrix.shape, F32),
        grid_spec=pltpu.PrefetchScalarGridSpec(
            num_scalar_prefetch=1,
            grid=(columns // width,),
            in_specs=[
                pl.BlockSpec(left.shape, lambda i, rank: (0, 0)),
                pl.BlockSpec(keep.shape, lambda i, rank: (0, 0)),
                pl.BlockSpec((rows, width), lambda i, rank: (0, i)),
                pl.BlockSpec((2, 1, 2 * NB, LANES), lambda i, rank: (i % 8, i // 8, 0, 0)),
                pl.BlockSpec((2, 2, 1, NB, LANES), lambda i, rank: (i % 8, 0, i // 8, 0, 0)),
            ],
            out_specs=pl.BlockSpec((rows, width), lambda i, rank: (0, i)),
        ),
        compiler_params=pltpu.CompilerParams(vmem_limit_bytes=VMEM_LIMIT),
        cost_estimate=pl.CostEstimate(
            flops=2 * rows * columns * left.shape[1], bytes_accessed=40 << 20, transcendentals=0
        ),
        name="update",
    )(rank, left, keep, matrix, upper, tops)


def body(matrix, lower_panels, inverses, pivots):
    rank = lax.axis_index("prow")
    column_rank = lax.axis_index("pcol")
    y, z, core = rank // 8, rank // 2 % 4, rank % 2
    rows = matrix.shape[0]
    index = jnp.arange(NB, dtype=jnp.int32)

    pivot0, pivot1 = pivots[0], pivots[1]
    again = pivot1[:, None] == pivot0[None, :]
    from_top = jnp.any(again, axis=1)
    source1 = jnp.where(from_top, jnp.sum(jnp.where(again, index[None, :], 0), axis=1), pivot1)
    sources = jnp.concatenate([pivot0, source1])

    def local(matrix_row):
        blocks = matrix_row // NB
        place = blocks // 32 * NB + matrix_row % NB
        return jnp.where(blocks % 32 == rank, place, -1)

    local_row = jnp.arange(rows, dtype=jnp.int32)
    select = (local(sources)[:, None] == local_row[None, :]).astype(BF16)

    keep_place = jnp.stack([core, y, z]).astype(jnp.int32)
    send_place = jnp.stack([1 - core, y, z]).astype(jnp.int32)
    sent = pick_rows(send_place, select, matrix)
    other = [lax.ppermute(value, "prow", SWAP_CORES) for value in sent]
    kept = pick_rows(keep_place, select, matrix)
    part_a = [kept[0][d] + other[0][d] for d in range(4)]
    part_b = [kept[1][d] + other[1][d] for d in range(4)]

    def add_up(parts, axis):
        total = parts[0]
        for d in (1, 3, 2):
            total = total + shift(parts[d], **{axis: d})
        return total

    part_a = add_up(part_a, "dz")
    part_b = add_up(part_b, "dy")
    raw0 = add_up([part_a[d] for d in range(4)], "dy")
    raw1 = add_up([part_b[d] for d in range(4)], "dz")

    def panel_select(matrix_row):
        blocks = matrix_row // NB
        place = blocks // 32 * NB + matrix_row % NB
        piece = lower_panels.shape[1]
        mine = (blocks % 32 == rank) & (place // piece == column_rank)
        place = jnp.where(mine, place % piece, -1)
        return (place[:, None] == jnp.arange(piece, dtype=jnp.int32)[None, :]).astype(F32)

    panel_rows = jnp.concatenate([pivot1, NB + index])
    picked = jnp.dot(panel_select(panel_rows), lower_panels[0], precision=HIGHEST)
    picked = lax.psum(picked, ("prow", "pcol"))
    lower_pivot, lower_top = picked[:NB], picked[NB:]

    upper = solve(raw0, raw1, inverses, lower_pivot)
    upper = lax.all_gather(upper, "prow", axis=0).reshape(16, 2, 2 * NB, LANES)

    tops = scatter_tops(matrix, y, z)
    tops = lax.all_gather(tops, "prow", axis=0).reshape(16, 2, 2, NB, LANES)

    pieces = [lower_panels] + [
        lax.ppermute(lower_panels, "pcol", [(i, (i + d) % 4) for i in range(4)]) for d in (1, 2, 3)
    ]
    pieces = jnp.stack(pieces)
    order = (column_rank - jnp.arange(4, dtype=jnp.int32)) % 4
    pieces = pieces[order]
    lower0 = pieces[:, 0].reshape(rows, NB)
    lower1 = pieces[:, 1].reshape(rows, NB)

    takes0 = (pivot0 >= 2 * NB) & ~jnp.any(again, axis=0)
    place0 = jnp.where(takes0, local(pivot0), -1)
    place1 = local(pivot1)
    hit0 = local_row[:, None] == place0[None, :]
    hit1 = local_row[:, None] == place1[None, :]
    moved = (NB + index)[:, None] == pivot0[None, :]
    top1 = jnp.where(
        jnp.any(moved, axis=1),
        jnp.sum(jnp.where(moved, index[None, :], 0), axis=1),
        NB + index,
    )
    to_top = (top1[:, None] == jnp.arange(2 * NB, dtype=jnp.int32)[None, :]).astype(BF16)
    take = jnp.dot(hit1.astype(BF16), to_top, preferred_element_type=F32)
    take = take + jnp.concatenate([hit0, jnp.zeros_like(hit0)], axis=1).astype(F32)
    second = jnp.any(hit1, axis=1)[:, None]
    replaced = second | jnp.any(hit0, axis=1)[:, None]
    lower0 = jnp.where(second, jnp.dot(hit1.astype(F32), lower_top, precision=HIGHEST), lower0)
    lower = -jnp.concatenate([lower0, lower1], axis=1)
    high = lax.reduce_precision(lower, 8, 7)
    low = (lower - high).astype(BF16)
    high = high.astype(BF16)
    take = take.astype(BF16)
    left = jnp.concatenate([high, high, low, take, take], axis=1)
    keep = jnp.where(replaced, 0.0, 1.0).astype(F32)
    return update(rank.reshape(1).astype(jnp.int32), left, keep, matrix, upper, tops)


def solution(mesh):
    placed = (P("prow", "pcol"), P(None, ("prow", "pcol"), None), P(), P())
    return jax.shard_map(
        body, mesh=mesh, in_specs=placed, out_specs=P("prow", "pcol"), check_vma=False
    )
```

```python
import jax
import jax.numpy as jnp
from jax import lax
from jax.experimental import pallas as pl
from jax.experimental.pallas import tpu as pltpu
from jax.sharding import PartitionSpec as P

F32 = jnp.float32
BF16 = jnp.bfloat16
HIGHEST = lax.Precision.HIGHEST
NB = 256
LANES = 128
SHARE = 2 * NB + 32
VMEM_LIMIT = 56 * 1024 * 1024


def rank_of(y, z, core):
    return ((y % 4) * 4 + z % 4) * 2 + core


def moved(y, z, core, one, two):
    return (y + two, z + one, core) if core == 0 else (y + one, z + two, core)


def send(value, one=0, two=0, only=lambda one, two: True):
    pairs = []
    for y in range(4):
        for z in range(4):
            for core in range(2):
                at = (z, y) if core == 0 else (y, z)
                if only(*at):
                    pairs.append((rank_of(y, z, core), rank_of(*moved(y, z, core, one, two))))
    return lax.ppermute(value, "prow", pairs)


def swap_cores(value):
    return lax.ppermute(value, "prow", [(rank, rank ^ 1) for rank in range(32)])


def split_two(value):
    high = value.astype(BF16)
    low = (value - high.astype(F32)).astype(BF16)
    return high, low


def exact_dot(a, b):
    return jnp.dot(a, b, precision=HIGHEST, preferred_element_type=F32)


def chip_at(place, one, two):
    by_z = (place[1] + two) % 4 * 4 + (place[2] + one) % 4
    by_y = (place[1] + one) % 4 * 4 + (place[2] + two) % 4
    return jnp.where(place[0] == 0, by_z, by_y)


def pick_kernel(place_ref, select_ref, *refs):
    extras, blocks, out_ref = refs[:4], refs[4:8], refs[8]
    high, low = split_two(jnp.concatenate([block[...] for block in blocks], axis=1))
    select = select_ref[...]
    rows = jnp.dot(select, high, preferred_element_type=F32)
    rows = rows + jnp.dot(select, low, preferred_element_type=F32)
    for two in range(4):
        out_ref[0, two, : 2 * NB] = rows[:, two * LANES : (two + 1) * LANES]
        out_ref[0, two, 2 * NB :] = extras[two][0]


def pick_rows(place, select, extra, matrix):
    def share(two):
        return lambda i, place: chip_at(place, i, two) * 2 + place[0]

    def columns(two):
        return pl.BlockSpec((matrix.shape[0], LANES), lambda i, place: (0, share(two)(i, place)))

    def extras(two):
        return pl.BlockSpec((1, 32, LANES), lambda i, place: (share(two)(i, place), 0, 0))

    return pl.pallas_call(
        pick_kernel,
        out_shape=jax.ShapeDtypeStruct((4, 4, SHARE, LANES), F32),
        grid_spec=pltpu.PrefetchScalarGridSpec(
            num_scalar_prefetch=1,
            grid=(4,),
            in_specs=[pl.BlockSpec(select.shape, lambda i, place: (0, 0))]
            + [extras(two) for two in range(4)]
            + [columns(two) for two in range(4)],
            out_specs=pl.BlockSpec((1, 4, SHARE, LANES), lambda i, place: (i, 0, 0, 0)),
        ),
        compiler_params=pltpu.CompilerParams(vmem_limit_bytes=VMEM_LIMIT),
        cost_estimate=pl.CostEstimate(
            flops=2 * 2 * 512 * 768 * 2048, bytes_accessed=10 << 20, transcendentals=0
        ),
        name="pick_rows",
    )(place, select, *([extra] * 4), *([matrix] * 4))


def cut_kernel(place_ref, *refs):
    blocks, outs = refs[:4], refs[4:]
    for one in range(4):

        @pl.when(pl.program_id(0) == one)
        def _(one=one):
            for two in range(4):
                outs[one][two] = blocks[two][...]


def cut_top(place, matrix):
    def block(two):
        return pl.BlockSpec((NB, 2 * LANES), lambda i, place: (0, chip_at(place, i, two)))

    return pl.pallas_call(
        cut_kernel,
        out_shape=tuple(jax.ShapeDtypeStruct((4, NB, 2 * LANES), F32) for _ in range(4)),
        grid_spec=pltpu.PrefetchScalarGridSpec(
            num_scalar_prefetch=1,
            grid=(4,),
            in_specs=[block(two) for two in range(4)],
            out_specs=tuple(
                pl.BlockSpec((4, NB, 2 * LANES), lambda i, place: (0, 0, 0)) for _ in range(4)
            ),
        ),
        compiler_params=pltpu.CompilerParams(vmem_limit_bytes=VMEM_LIMIT),
        cost_estimate=pl.CostEstimate(flops=0, bytes_accessed=8 << 20, transcendentals=0),
        name="cut_top",
    )(place, *([matrix] * 4))


def solve_kernel(raw_ref, inverse_ref, out_ref):
    out_ref[:NB] = exact_dot(inverse_ref[0], raw_ref[:NB])
    out_ref[NB : 2 * NB] = exact_dot(inverse_ref[1], raw_ref[NB : 2 * NB])
    out_ref[2 * NB :] = raw_ref[2 * NB :]


def solve(raw, inverses):
    return pl.pallas_call(
        solve_kernel,
        out_shape=jax.ShapeDtypeStruct((SHARE, LANES), F32),
        cost_estimate=pl.CostEstimate(
            flops=6 * 2 * 2 * 256 * 256 * 128, bytes_accessed=1 << 20, transcendentals=0
        ),
        name="solve",
    )(raw, inverses)


def update_kernel(
    place_ref, keep_ref, take_ref, hit_ref, lower_ref, inverse_ref,
    matrix_ref, top_ref, *refs,
):
    pieces, extras = refs[:16], refs[16:32]
    out_ref, left_ref, upper_ref, flat_ref = refs[32:]
    core, rank = place_ref[0], place_ref[3]
    step = pl.program_id(0)

    @pl.when(step == 0)
    def _():
        for side in range(2):
            for turn in range(4):
                for inner in range(4):
                    one, two = (turn, inner) if side == 0 else (inner, turn)
                    owner = chip_at(place_ref, one, two) * 2 + (core + side) % 2
                    start = pl.multiple_of(owner * 32, 32)
                    slot = side * 8 + turn * 2 + inner // 2
                    flat_ref[pl.ds(start, 32)] = extras[slot][inner % 2]
        pivot_rows = jnp.concatenate([flat_ref[:NB], flat_ref[2 * NB : 3 * NB]], axis=1)
        top_rows = jnp.concatenate([flat_ref[NB : 2 * NB], flat_ref[3 * NB :]], axis=1)
        weight = exact_dot(inverse_ref[1], pivot_rows)
        hit = hit_ref[...].astype(F32)
        swapped = jnp.max(hit, axis=1, keepdims=True) > 0.0
        lower0 = jnp.where(swapped, exact_dot(hit, top_rows), lower_ref[0])
        lower1 = lower_ref[1]
        lower0 = lower0 - exact_dot(lower1, weight)
        at_second = rank == 1
        lower0 = jnp.concatenate([jnp.where(at_second, weight, lower0[:NB]), lower0[NB:]], axis=0)
        lower1 = jnp.concatenate([jnp.where(at_second, 0.0, lower1[:NB]), lower1[NB:]], axis=0)
        high, low = split_two(-jnp.concatenate([lower0, lower1], axis=1))
        take = take_ref[...]
        for i, part in enumerate((high, high, low, take, take)):
            left_ref[:, i * 2 * NB : (i + 1) * 2 * NB] = part

    for side, turn, inner in ((0, step // 4, step % 4), (1, step % 4, step // 4)):
        lanes = pl.ds(pl.multiple_of((core + side) % 2 * LANES, LANES), LANES)
        for slot in range(8):

            @pl.when((turn == slot // 2) & (inner // 2 == slot % 2))
            def _(slot=slot, side=side, lanes=lanes):
                upper_ref[:, lanes] = pieces[side * 8 + slot][0, : 2 * NB]

    upper = upper_ref[...]
    tops = jnp.concatenate([top_ref[0, 0], top_ref[0, 1]], axis=0)
    upper_high, upper_low = split_two(upper)
    top_high, top_low = split_two(tops)
    right = jnp.concatenate([upper_high, upper_low, upper_high, top_high, top_low], axis=0)
    total = jnp.dot(left_ref[...], right, preferred_element_type=F32)
    out_ref[...] = matrix_ref[...] * keep_ref[...] + total

    @pl.when(rank == 0)
    def _():
        out_ref[:NB] = upper[:NB]

    @pl.when(rank == 1)
    def _():
        out_ref[:NB] = out_ref[:NB] + upper[NB:]


def update(place, keep, take, hit, lower, inverse, matrix, tops, pieces):
    rows, columns = matrix.shape
    width = 2 * LANES

    def whole(array):
        return pl.BlockSpec(array.shape, lambda i, place: (0,) * array.ndim)

    def chip(i, place):
        return chip_at(place, i // 4, i % 4)

    def piece_spec(side, slot):
        def own(i, place):
            return (jnp.clip(i - 2 * slot, 0, 1), 0, 0)

        def other(i, place):
            return (jnp.clip(i // 4 - slot % 2 * 2, 0, 1), 0, 0)

        return pl.BlockSpec((1, SHARE, LANES), other if side else own)

    extra_spec = pl.BlockSpec((2, 32, LANES), lambda i, place: (0, 16, 0))
    pieces = list(pieces)
    return pl.pallas_call(
        update_kernel,
        out_shape=jax.ShapeDtypeStruct(matrix.shape, F32),
        grid_spec=pltpu.PrefetchScalarGridSpec(
            num_scalar_prefetch=1,
            grid=(columns // width,),
            in_specs=[whole(a) for a in (keep, take, hit, lower, inverse)]
            + [
                pl.BlockSpec((rows, width), lambda i, place: (0, chip(i, place))),
                pl.BlockSpec((1, 2, NB, width), lambda i, place: (chip(i, place), 0, 0, 0)),
            ]
            + [piece_spec(side, slot) for side in range(2) for slot in range(8)]
            + [extra_spec] * 16,
            out_specs=pl.BlockSpec((rows, width), lambda i, place: (0, chip(i, place))),
            scratch_shapes=[
                pltpu.VMEM((rows, 10 * NB), BF16),
                pltpu.VMEM((2 * NB, width), F32),
                pltpu.VMEM((4 * NB, LANES), F32),
            ],
        ),
        compiler_params=pltpu.CompilerParams(vmem_limit_bytes=VMEM_LIMIT),
        cost_estimate=pl.CostEstimate(
            flops=2 * rows * columns * 10 * NB, bytes_accessed=40 << 20, transcendentals=0
        ),
        name="update",
    )(place, keep, take, hit, lower, inverse, matrix, tops, *pieces, *pieces)


def body(matrix, lower_panels, inverses, pivots):
    rank = lax.axis_index("prow")
    column_rank = lax.axis_index("pcol")
    y, z, core = rank // 8, rank // 2 % 4, rank % 2
    first = jnp.where(core == 0, z, y)
    second = jnp.where(core == 0, y, z)
    rows = matrix.shape[0]
    index = jnp.arange(NB, dtype=jnp.int32)
    place = jnp.stack([core, y, z, rank]).astype(jnp.int32)
    other_place = jnp.stack([1 - core, y, z, rank]).astype(jnp.int32)

    panel = lower_panels[0]
    far = [lax.ppermute(panel, "pcol", [(i, (i - d) % 4) for i in range(4)]) for d in (1, 2, 3)]
    panel = jnp.concatenate([panel] + far)

    top_parts = cut_top(place, matrix)
    top_got = [
        send(top_parts[d], one=d, only=lambda one, two: one == 0 and two == 0) for d in (2, 1, 3)
    ]

    pivot0, pivot1 = pivots[0], pivots[1]
    again = pivot1[:, None] == pivot0[None, :]
    from_top = jnp.any(again, axis=1)
    source1 = jnp.where(from_top, jnp.sum(jnp.where(again, index[None, :], 0), axis=1), pivot1)
    sources = jnp.concatenate([pivot0, source1])

    def local(matrix_row):
        blocks = matrix_row // NB
        where = blocks // 32 * NB + matrix_row % NB
        return jnp.where(blocks % 32 == rank, where, -1)

    local_row = jnp.arange(rows, dtype=jnp.int32)
    select = (local(sources)[:, None] == local_row[None, :]).astype(BF16)

    panel_rows = jnp.concatenate([pivot1, NB + index])
    piece = lower_panels.shape[1]
    where = local(panel_rows)
    away = (where // piece - column_rank) % 4 * piece + where % piece
    where = jnp.where(where >= 0, away, -1)
    extra = exact_dot((where[:, None] == local_row[None, :]).astype(F32), panel)
    extra = jnp.concatenate([extra[:, :LANES], extra[:, LANES:]], axis=0).reshape(32, 32, LANES)

    sent = pick_rows(other_place, select, extra, matrix)
    other = swap_cores(sent)
    own_place, _ = lax.optimization_barrier((place, sent))
    kept = pick_rows(own_place, select, extra, matrix)
    part = [kept[d] + other[d] for d in range(4)]
    ahead = send(part[2][:2], one=1)
    behind = send(part[2][2:], one=3)
    part[1] = jnp.concatenate([part[1][:2] + ahead, part[1][2:]])
    part[3] = jnp.concatenate([part[3][:2], part[3][2:] + behind])
    part = part[0] + send(part[1], one=1) + send(part[3], one=3)
    top_got, _ = lax.optimization_barrier((top_got, kept))
    top_held = jnp.where(first == 0, top_parts[0], top_got[0] + top_got[1] + top_got[2])
    top_got = [send(top_held[d], two=d, only=lambda one, two: two == 0) for d in (2, 1, 3)]
    top_share = jnp.where(second == 0, top_held[0], top_got[0] + top_got[1] + top_got[2])
    top_share, part = lax.optimization_barrier((top_share, part))
    tops = lax.all_gather(top_share, "prow", axis=0).reshape(16, 2, NB, 2 * LANES)

    lower = lax.all_gather(lower_panels, "pcol", axis=1, tiled=True)

    takes0 = (pivot0 >= 2 * NB) & ~jnp.any(again, axis=0)
    place0 = jnp.where(takes0, local(pivot0), -1)
    hit0 = local_row[:, None] == place0[None, :]
    hit1 = local_row[:, None] == local(pivot1)[None, :]
    shifted = (NB + index)[:, None] == pivot0[None, :]
    top1 = jnp.where(
        jnp.any(shifted, axis=1),
        jnp.sum(jnp.where(shifted, index[None, :], 0), axis=1),
        NB + index,
    )
    to_top = (top1[:, None] == jnp.arange(2 * NB, dtype=jnp.int32)[None, :]).astype(BF16)
    hit1 = hit1.astype(BF16)
    take = jnp.dot(hit1, to_top, preferred_element_type=F32)
    take = take + jnp.concatenate([hit0, jnp.zeros_like(hit0)], axis=1).astype(F32)
    replaced = jnp.any(hit1 > 0, axis=1) | jnp.any(hit0, axis=1)
    replaced = replaced | ((rank == 1) & (local_row < NB))
    keep = jnp.where(replaced, 0.0, 1.0).astype(F32)[:, None]
    take = take.astype(BF16)

    raw = part[0]
    for d in (2, 1, 3):
        raw = raw + send(part[d], two=d)

    raw, keep, take, hit1, lower = lax.optimization_barrier((raw, keep, take, hit1, lower))
    share = solve(raw, inverses)

    near = {d: send(share, two=4 - d) for d in (1, 2, 3)}
    low = jnp.stack([share, near[1]])
    high = jnp.stack([near[2], near[3]])
    low_before, high_after = send(low, one=1), send(high, one=3)
    high_before, low_after = send(high, one=1), send(low, one=3)
    low_across, high_across = send(low_before, one=1), send(high_after, one=3)
    pieces = [
        low, high, low_after, high_after, low_across, high_across, low_before, high_before
    ]
    pieces = pieces + [swap_cores(value) for value in pieces]
    return update(place, keep, take, hit1, lower, inverses, matrix, tops, pieces)


def solution(mesh):
    placed = (P("prow", "pcol"), P(None, ("prow", "pcol"), None), P(), P())
    return jax.shard_map(
        body, mesh=mesh, in_specs=placed, out_specs=P("prow", "pcol"), check_vma=False
    )
```

```python
import jax
import jax.numpy as jnp
from jax import lax
from jax.experimental import pallas as pl
from jax.experimental.pallas import tpu as pltpu
from jax.sharding import PartitionSpec as P

F32 = jnp.float32
BF16 = jnp.bfloat16
HIGHEST = lax.Precision.HIGHEST
NB = 256
LANES = 128
EXTRA = 32
SHARE = 2 * NB + EXTRA
VMEM_LIMIT = 56 * 1024 * 1024


def rank_of(y, z, core):
    return ((y % 4) * 4 + z % 4) * 2 + core


def moved(y, z, core, one, two):
    return (y + two, z + one, core) if core == 0 else (y + one, z + two, core)


def send(value, one=0, two=0, only=lambda one, two: True):
    pairs = []
    for y in range(4):
        for z in range(4):
            for core in range(2):
                at = (z, y) if core == 0 else (y, z)
                if only(*at):
                    pairs.append((rank_of(y, z, core), rank_of(*moved(y, z, core, one, two))))
    return lax.ppermute(value, "prow", pairs)


def swap_cores(value):
    return lax.ppermute(value, "prow", [(rank, rank ^ 1) for rank in range(32)])


def split_two(value):
    high = value.astype(BF16)
    low = (value - high.astype(F32)).astype(BF16)
    return high, low


def exact_dot(a, b):
    return jnp.dot(a, b, precision=HIGHEST, preferred_element_type=F32)


def chip_at(place, one, two):
    by_z = (place[1] + two) % 4 * 4 + (place[2] + one) % 4
    by_y = (place[1] + one) % 4 * 4 + (place[2] + two) % 4
    return jnp.where(place[0] == 0, by_z, by_y)


def pick_kernel(place_ref, matrix_ref, select_ref, out_ref, left_ref, blocks_ref, rows_ref, in_sems, out_sems):
    def fetches(one):
        return [
            pltpu.make_async_copy(
                matrix_ref.at[:, pl.ds(pl.multiple_of(share * LANES, LANES), LANES)],
                blocks_ref.at[one, :, pl.ds(two * LANES, LANES)],
                in_sems.at[one, two],
            )
            for two in range(4)
            for share in [chip_at(place_ref, one, two) * 2 + place_ref[0]]
        ]

    def store(one):
        return pltpu.make_async_copy(rows_ref.at[one], out_ref.at[one], out_sems.at[one])

    for one in range(4):
        for copy in fetches(one):
            copy.start()
    for part in range(2):
        left_ref[:, part * select_ref.shape[1] : (part + 1) * select_ref.shape[1]] = select_ref[...]

    @pl.loop(0, 4)
    def _(one):
        for copy in fetches(one):
            copy.wait()
        right = jnp.concatenate(split_two(blocks_ref[one]), axis=0)
        rows = jnp.dot(left_ref[...], right, preferred_element_type=F32)
        for two in range(4):
            rows_ref[one, two] = rows[:, two * LANES : (two + 1) * LANES]
        store(one).start()

    for one in range(4):
        store(one).wait()


def pick_rows(place, select, matrix):
    rows = matrix.shape[0]
    hbm = pl.BlockSpec(memory_space=pl.ANY)
    shape = (4, 4, 2 * NB, LANES)
    return pl.pallas_call(
        pick_kernel,
        out_shape=jax.ShapeDtypeStruct(shape, F32),
        in_specs=[
            pl.BlockSpec(memory_space=pltpu.SMEM), hbm, pl.BlockSpec(memory_space=pltpu.VMEM)
        ],
        out_specs=hbm,
        scratch_shapes=[
            pltpu.VMEM((2 * NB, 2 * rows), BF16),
            pltpu.VMEM((4, rows, 4 * LANES), F32),
            pltpu.VMEM(shape, F32),
            pltpu.SemaphoreType.DMA((4, 4)),
            pltpu.SemaphoreType.DMA((4,)),
        ],
        compiler_params=pltpu.CompilerParams(vmem_limit_bytes=52 << 20),
        cost_estimate=pl.CostEstimate(
            flops=2 * 2 * 512 * 768 * 2048, bytes_accessed=10 << 20, transcendentals=0
        ),
        name="pick_rows",
    )(place, matrix, select)


def extra_kernel(place_ref, select_ref, own_ref, other_ref, out_ref, flat_ref):
    total = None
    for part, lower_ref in enumerate((own_ref, other_ref)):
        lower = lower_ref[...]
        high, rest = split_two(lower)
        middle, low = split_two(lower - high.astype(F32))
        select = select_ref[part]
        for piece in (high, middle, low):
            rows = jnp.dot(select, piece, preferred_element_type=F32)
            total = rows if total is None else total + rows
    flat_ref[: 2 * NB] = total[:, :LANES]
    flat_ref[2 * NB :] = total[:, LANES:]
    for one in range(4):
        for two in range(4):
            share = chip_at(place_ref, one, two) * 2 + place_ref[0]
            start = pl.multiple_of(share * EXTRA, EXTRA)
            out_ref[one, two] = flat_ref[pl.ds(start, EXTRA)]


def pick_extra(place, select, own, other):
    return pl.pallas_call(
        extra_kernel,
        out_shape=jax.ShapeDtypeStruct((4, 4, EXTRA, LANES), F32),
        in_specs=[pl.BlockSpec(memory_space=pltpu.SMEM)]
        + [pl.BlockSpec(memory_space=pltpu.VMEM)] * 3,
        scratch_shapes=[pltpu.VMEM((4 * NB, LANES), F32)],
        compiler_params=pltpu.CompilerParams(vmem_limit_bytes=16 << 20),
        cost_estimate=pl.CostEstimate(
            flops=2 * 3 * 512 * 1536 * 256, bytes_accessed=4 << 20, transcendentals=0
        ),
        name="pick_extra",
    )(place, select, own, other)


def solve_kernel(raw_ref, inverse_ref, out_ref):
    out_ref[:NB] = exact_dot(inverse_ref[0], raw_ref[:NB])
    out_ref[NB : 2 * NB] = exact_dot(inverse_ref[1], raw_ref[NB : 2 * NB])
    out_ref[2 * NB :] = raw_ref[2 * NB :]


def solve(raw, inverses):
    return pl.pallas_call(
        solve_kernel,
        out_shape=jax.ShapeDtypeStruct((SHARE, LANES), F32),
        cost_estimate=pl.CostEstimate(
            flops=6 * 2 * 2 * 256 * 256 * 128, bytes_accessed=1 << 20, transcendentals=0
        ),
        name="solve",
    )(raw, inverses)


def tops_kernel(
    matrix_ref, top_ref, take_ref, out_ref, left_ref, tops_ref, blocks_ref, in_sems, out_sems
):
    width = 2 * LANES

    def lanes(step):
        return pl.ds(pl.multiple_of(step * width, width), width)

    def fetches(step):
        return (
            pltpu.make_async_copy(top_ref.at[:, lanes(step)], tops_ref.at[step], in_sems.at[0, step]),
            pltpu.make_async_copy(
                matrix_ref.at[:, lanes(step)], blocks_ref.at[step], in_sems.at[1, step]
            ),
        )

    def store(step):
        return pltpu.make_async_copy(
            blocks_ref.at[step], out_ref.at[:, lanes(step)], out_sems.at[step]
        )

    @pl.loop(0, 16)
    def _(step):
        for copy in fetches(step):
            copy.start()

    left_ref[:, : 2 * NB] = take_ref[...]
    left_ref[:, 2 * NB :] = take_ref[...]

    @pl.loop(0, 16)
    def _(step):
        for copy in fetches(step):
            copy.wait()
        high, low = split_two(tops_ref[step])
        right = jnp.concatenate([high, low], axis=0)
        total = jnp.dot(left_ref[...], right, preferred_element_type=F32)
        blocks_ref[step] = blocks_ref[step] + total
        store(step).start()

    @pl.loop(0, 16)
    def _(step):
        store(step).wait()


def put_tops(matrix, tops, take):
    rows = matrix.shape[0]
    hbm = pl.BlockSpec(memory_space=pl.ANY)
    vmem = pl.BlockSpec(memory_space=pltpu.VMEM)
    return pl.pallas_call(
        tops_kernel,
        out_shape=jax.ShapeDtypeStruct(matrix.shape, F32),
        in_specs=[hbm, hbm, vmem],
        out_specs=hbm,
        input_output_aliases={0: 0},
        scratch_shapes=[
            pltpu.VMEM((rows, 4 * NB), BF16),
            pltpu.VMEM((16, 2 * NB, 2 * LANES), F32),
            pltpu.VMEM((16, rows, 2 * LANES), F32),
            pltpu.SemaphoreType.DMA((2, 16)),
            pltpu.SemaphoreType.DMA((16,)),
        ],
        compiler_params=pltpu.CompilerParams(vmem_limit_bytes=52 << 20),
        cost_estimate=pl.CostEstimate(
            flops=2 * rows * 4096 * 4 * NB, bytes_accessed=32 << 20, transcendentals=0
        ),
        name="put_tops",
    )(matrix, tops, take)


def update_kernel(place_ref, source_ref, keep_ref, hit_ref, lower_ref, inverse_ref, *refs):
    pieces = refs[:16]
    out_ref, left_ref, held_ref, flat_ref, blocks_ref, piece_sems, in_sems, out_sems = refs[16:]
    core, rank = place_ref[0], place_ref[3]
    width = 2 * LANES
    copies = [
        pltpu.make_async_copy(
            pieces[side * 8 + slot],
            held_ref.at[side, slot // 2, pl.ds(slot % 2 * 2, 2)],
            piece_sems.at[side * 8 + slot],
        )
        for side in range(2)
        for slot in range(8)
    ]
    for copy in copies:
        copy.start()

    def lanes(step):
        chip = chip_at(place_ref, step // 4, step % 4)
        return pl.ds(pl.multiple_of(chip * width, width), width)

    def fetch(step):
        return pltpu.make_async_copy(
            source_ref.at[:, lanes(step)], blocks_ref.at[step], in_sems.at[step]
        )

    def store(step):
        return pltpu.make_async_copy(
            blocks_ref.at[step], out_ref.at[:, lanes(step)], out_sems.at[step]
        )

    @pl.loop(0, 16)
    def _(step):
        fetch(step).start()

    for copy in copies:
        copy.wait()
    for side in range(2):
        for turn in range(4):
            for inner in range(4):
                one, two = (turn, inner) if side == 0 else (inner, turn)
                owner = chip_at(place_ref, one, two) * 2 + (core + side) % 2
                start = pl.multiple_of(owner * EXTRA, EXTRA)
                flat_ref[pl.ds(start, EXTRA)] = held_ref[side, turn, inner, 2 * NB :]
    pivot_rows = jnp.concatenate([flat_ref[:NB], flat_ref[2 * NB : 3 * NB]], axis=1)
    top_rows = jnp.concatenate([flat_ref[NB : 2 * NB], flat_ref[3 * NB :]], axis=1)
    weight = exact_dot(inverse_ref[1], pivot_rows)
    hit = hit_ref[...].astype(F32)
    swapped = jnp.max(hit, axis=1, keepdims=True) > 0.0
    lower0 = jnp.where(swapped, exact_dot(hit, top_rows), lower_ref[0])
    lower1 = lower_ref[1]
    lower0 = lower0 - exact_dot(lower1, weight)
    at_second = rank == 1
    lower0 = jnp.concatenate([jnp.where(at_second, weight, lower0[:NB]), lower0[NB:]], axis=0)
    lower1 = jnp.concatenate([jnp.where(at_second, 0.0, lower1[:NB]), lower1[NB:]], axis=0)
    high, low = split_two(-jnp.concatenate([lower0, lower1], axis=1))
    for i, part in enumerate((high, high, low)):
        left_ref[:, i * 2 * NB : (i + 1) * 2 * NB] = part

    @pl.loop(0, 16)
    def _(step):
        own = held_ref[0, step // 4, step % 4, : 2 * NB]
        other = held_ref[1, step % 4, step // 4, : 2 * NB]
        upper = jnp.concatenate(
            [jnp.where(core == 0, own, other), jnp.where(core == 0, other, own)], axis=1
        )
        fetch(step).wait()
        high, low = split_two(upper)
        right = jnp.concatenate([high, low, high], axis=0)
        total = jnp.dot(left_ref[...], right, preferred_element_type=F32)
        total = blocks_ref[step] * keep_ref[...] + total
        start = jnp.where(at_second, total[:NB] + upper[NB:], total[:NB])
        blocks_ref[step, :NB] = jnp.where(rank == 0, upper[:NB], start)
        blocks_ref[step, NB:] = total[NB:]
        store(step).start()

    @pl.loop(0, 16)
    def _(step):
        store(step).wait()


def update(place, source, keep, hit, lower, inverse, pieces):
    rows, columns = source.shape
    hbm = pl.BlockSpec(memory_space=pl.ANY)
    vmem = pl.BlockSpec(memory_space=pltpu.VMEM)
    return pl.pallas_call(
        update_kernel,
        out_shape=jax.ShapeDtypeStruct(source.shape, F32),
        in_specs=[pl.BlockSpec(memory_space=pltpu.SMEM), hbm] + [vmem] * 4 + [hbm] * 16,
        out_specs=hbm,
        scratch_shapes=[
            pltpu.VMEM((rows, 6 * NB), BF16),
            pltpu.VMEM((2, 4, 4, SHARE, LANES), F32),
            pltpu.VMEM((4 * NB, LANES), F32),
            pltpu.VMEM((16, rows, 2 * LANES), F32),
            pltpu.SemaphoreType.DMA((16,)),
            pltpu.SemaphoreType.DMA((16,)),
            pltpu.SemaphoreType.DMA((16,)),
        ],
        compiler_params=pltpu.CompilerParams(vmem_limit_bytes=52 << 20),
        cost_estimate=pl.CostEstimate(
            flops=2 * rows * columns * 6 * NB, bytes_accessed=33 << 20, transcendentals=0
        ),
        name="update",
    )(place, source, keep, hit, lower, inverse, *pieces)


def own_tops_kernel(place_ref, matrix_ref, out_ref, zero_ref, held_ref, sems, zero_sems):
    rank = place_ref[3]
    zero_ref[...] = jnp.zeros_like(zero_ref)
    width = zero_ref.shape[1]

    def blanks(panel):
        return [
            pltpu.make_async_copy(
                zero_ref,
                out_ref.at[pl.ds(panel * NB, NB), pl.ds(i * width, width)],
                zero_sems.at[panel, i],
            )
            for i in range(4)
        ]

    for panel in range(2):

        @pl.when(rank != panel)
        def _(panel=panel):
            for copy in blanks(panel):
                copy.start()

    for panel in range(2):

        @pl.when(rank == panel)
        def _(panel=panel):
            load = pltpu.make_async_copy(matrix_ref.at[pl.ds(0, NB)], held_ref, sems.at[0])
            load.start()
            load.wait()
            store = pltpu.make_async_copy(
                held_ref, out_ref.at[pl.ds(panel * NB, NB)], sems.at[1]
            )
            store.start()
            store.wait()

    for panel in range(2):

        @pl.when(rank != panel)
        def _(panel=panel):
            for copy in blanks(panel):
                copy.wait()


def own_tops(place, matrix):
    columns = matrix.shape[1]
    hbm = pl.BlockSpec(memory_space=pl.ANY)
    return pl.pallas_call(
        own_tops_kernel,
        out_shape=jax.ShapeDtypeStruct((2 * NB, columns), F32),
        in_specs=[pl.BlockSpec(memory_space=pltpu.SMEM), hbm],
        out_specs=hbm,
        scratch_shapes=[
            pltpu.VMEM((NB, columns // 4), F32),
            pltpu.VMEM((NB, columns), F32),
            pltpu.SemaphoreType.DMA((2,)),
            pltpu.SemaphoreType.DMA((2, 4)),
        ],
        compiler_params=pltpu.CompilerParams(vmem_limit_bytes=VMEM_LIMIT),
        cost_estimate=pl.CostEstimate(flops=0, bytes_accessed=8 << 20, transcendentals=0),
        name="own_tops",
    )(place, matrix)


def body(matrix, lower_panels, inverses, pivots):
    rank = lax.axis_index("prow")
    column_rank = lax.axis_index("pcol")
    y, z, core = rank // 8, rank // 2 % 4, rank % 2
    first = jnp.where(core == 0, z, y)
    second = jnp.where(core == 0, y, z)
    rows = matrix.shape[0]
    index = jnp.arange(NB, dtype=jnp.int32)
    place = jnp.stack([core, y, z, rank]).astype(jnp.int32)
    other_place = jnp.stack([1 - core, y, z, rank]).astype(jnp.int32)

    tops = lax.psum(own_tops(place, matrix), "prow")

    lower = lax.all_gather(lower_panels, "pcol", axis=1, tiled=True)
    lower_own = lower_panels[0]
    far = [lax.ppermute(lower_own, "pcol", [(i, (i - d) % 4) for i in range(4)]) for d in (1, 2, 3)]
    lower_own = jnp.concatenate([lower_own] + far)


    pivot0, pivot1 = pivots[0], pivots[1]
    again = pivot1[:, None] == pivot0[None, :]
    from_top = jnp.any(again, axis=1)
    source1 = jnp.where(from_top, jnp.sum(jnp.where(again, index[None, :], 0), axis=1), pivot1)
    sources = jnp.concatenate([pivot0, source1])

    def local(matrix_row, owner=rank):
        blocks = matrix_row // NB
        where = blocks // 32 * NB + matrix_row % NB
        return jnp.where(blocks % 32 == owner, where, -1)

    local_row = jnp.arange(rows, dtype=jnp.int32)
    select = (local(sources)[:, None] == local_row[None, :]).astype(BF16)

    panel_rows = jnp.concatenate([pivot1, NB + index])
    want = jnp.stack([local(panel_rows), local(panel_rows, rank ^ 1)])
    piece = lower_panels.shape[1]
    away = (want // piece - column_rank) % 4 * piece + want % piece
    want = jnp.where(want >= 0, away, -1)
    want = (want[:, :, None] == local_row[None, None, :]).astype(BF16)

    def exchange(turn, share):
        lower_other = swap_cores(jnp.where(turn == 0, lower_own, 0.0))
        sent = pick_rows(other_place + turn, select, matrix)
        own_place, sent = lax.optimization_barrier((place + turn, sent))
        other = swap_cores(sent)

        kept = pick_rows(own_place, select, matrix)
        extra = pick_extra(place, want, lower_own, lower_other)
        part = [jnp.concatenate([kept[d] + other[d], extra[d]], axis=1) for d in range(4)]
        ahead = send(part[2][:2], one=1)
        behind = send(part[2][2:], one=3)
        part[1] = jnp.concatenate([part[1][:2] + ahead, part[1][2:]])
        part[3] = jnp.concatenate([part[3][:2], part[3][2:] + behind])
        part = part[0] + send(part[1], one=1) + send(part[3], one=3)

        raw = part[0]
        for d in (2, 1, 3):
            raw = raw + send(part[d], two=d)

        return solve(raw, inverses)

    rounds = jnp.minimum(pivots[0, 0] + 1, 1)
    share = lax.fori_loop(0, rounds, exchange, jnp.zeros((SHARE, LANES), F32))

    near = {d: send(share, two=4 - d) for d in (1, 2, 3)}
    low = jnp.stack([share, near[1]])
    high = jnp.stack([near[2], near[3]])

    pivots, high = lax.optimization_barrier((pivots, high))
    pivot0, pivot1 = pivots[0], pivots[1]
    again = pivot1[:, None] == pivot0[None, :]
    takes0 = (pivot0 >= 2 * NB) & ~jnp.any(again, axis=0)
    place0 = jnp.where(takes0, local(pivot0), -1)
    hit0 = local_row[:, None] == place0[None, :]
    hit1 = local_row[:, None] == local(pivot1)[None, :]
    shifted = (NB + index)[:, None] == pivot0[None, :]
    top1 = jnp.where(
        jnp.any(shifted, axis=1),
        jnp.sum(jnp.where(shifted, index[None, :], 0), axis=1),
        NB + index,
    )
    to_top = (top1[:, None] == jnp.arange(2 * NB, dtype=jnp.int32)[None, :]).astype(BF16)
    hit1 = hit1.astype(BF16)
    take = jnp.dot(hit1, to_top, preferred_element_type=F32)
    take = take + jnp.concatenate([hit0, jnp.zeros_like(hit0)], axis=1).astype(F32)
    replaced = jnp.any(hit1 > 0, axis=1) | jnp.any(hit0, axis=1)
    replaced = replaced | ((rank == 1) & (local_row < NB))
    keep = jnp.where(replaced, 0.0, 1.0).astype(F32)[:, None]
    take = take.astype(BF16)


    low_before, high_after = send(low, one=1), send(high, one=3)
    high_before, low_after = send(high, one=1), send(low, one=3)
    low_across, high_across = send(low_before, one=1), send(high_after, one=3)
    pieces = [
        low, high, low_after, high_after, low_across, high_across, low_before, high_before
    ]
    pieces = pieces + [swap_cores(value) for value in pieces]
    result = update(place, matrix, keep, hit1, lower, inverses, pieces)
    return put_tops(result, tops, take)


def solution(mesh):
    placed = (P("prow", "pcol"), P(None, ("prow", "pcol"), None), P(), P())
    return jax.shard_map(
        body, mesh=mesh, in_specs=placed, out_specs=P("prow", "pcol"), check_vma=False
    )
```

```python
import jax
import jax.numpy as jnp
from jax import lax
from jax.experimental import pallas as pl
from jax.experimental.pallas import tpu as pltpu
from jax.sharding import PartitionSpec as P

F32 = jnp.float32
BF16 = jnp.bfloat16
HIGHEST = lax.Precision.HIGHEST
NB = 256
LANES = 128
EXTRA = 32
SHARE = 2 * NB + EXTRA
VMEM_LIMIT = 56 * 1024 * 1024


def rank_of(y, z, core):
    return ((y % 4) * 4 + z % 4) * 2 + core


def moved(y, z, core, one, two):
    return (y + two, z + one, core) if core == 0 else (y + one, z + two, core)


def send(value, one=0, two=0, only=lambda one, two: True):
    pairs = []
    for y in range(4):
        for z in range(4):
            for core in range(2):
                at = (z, y) if core == 0 else (y, z)
                if only(*at):
                    pairs.append((rank_of(y, z, core), rank_of(*moved(y, z, core, one, two))))
    return lax.ppermute(value, "prow", pairs)


def swap_cores(value):
    return lax.ppermute(value, "prow", [(rank, rank ^ 1) for rank in range(32)])


def split_two(value):
    high = value.astype(BF16)
    low = (value - high.astype(F32)).astype(BF16)
    return high, low


def exact_dot(a, b):
    return jnp.dot(a, b, precision=HIGHEST, preferred_element_type=F32)


def chip_at(place, one, two):
    by_z = (place[1] + two) % 4 * 4 + (place[2] + one) % 4
    by_y = (place[1] + one) % 4 * 4 + (place[2] + two) % 4
    return jnp.where(place[0] == 0, by_z, by_y)


def pick_kernel(place_ref, matrix_ref, select_ref, out_ref, left_ref, blocks_ref, rows_ref, in_sems, out_sems):
    def fetches(one):
        return [
            pltpu.make_async_copy(
                matrix_ref.at[:, pl.ds(pl.multiple_of(share * LANES, LANES), LANES)],
                blocks_ref.at[one, :, pl.ds(two * LANES, LANES)],
                in_sems.at[one, two],
            )
            for two in range(4)
            for share in [chip_at(place_ref, one, two) * 2 + place_ref[0]]
        ]

    def store(one):
        return pltpu.make_async_copy(rows_ref.at[one], out_ref.at[one], out_sems.at[one])

    for one in range(4):
        for copy in fetches(one):
            copy.start()
    for part in range(2):
        left_ref[:, part * select_ref.shape[1] : (part + 1) * select_ref.shape[1]] = select_ref[...]

    @pl.loop(0, 4)
    def _(one):
        for copy in fetches(one):
            copy.wait()
        right = jnp.concatenate(split_two(blocks_ref[one]), axis=0)
        rows = jnp.dot(left_ref[...], right, preferred_element_type=F32)
        for two in range(4):
            rows_ref[one, two] = rows[:, two * LANES : (two + 1) * LANES]
        store(one).start()

    for one in range(4):
        store(one).wait()


def pick_rows(place, select, matrix):
    rows = matrix.shape[0]
    hbm = pl.BlockSpec(memory_space=pl.ANY)
    shape = (4, 4, 2 * NB, LANES)
    return pl.pallas_call(
        pick_kernel,
        out_shape=jax.ShapeDtypeStruct(shape, F32),
        in_specs=[
            pl.BlockSpec(memory_space=pltpu.SMEM), hbm, pl.BlockSpec(memory_space=pltpu.VMEM)
        ],
        out_specs=hbm,
        scratch_shapes=[
            pltpu.VMEM((2 * NB, 2 * rows), BF16),
            pltpu.VMEM((4, rows, 4 * LANES), F32),
            pltpu.VMEM(shape, F32),
            pltpu.SemaphoreType.DMA((4, 4)),
            pltpu.SemaphoreType.DMA((4,)),
        ],
        compiler_params=pltpu.CompilerParams(vmem_limit_bytes=52 << 20),
        cost_estimate=pl.CostEstimate(
            flops=2 * 2 * 512 * 768 * 2048, bytes_accessed=10 << 20, transcendentals=0
        ),
        name="pick_rows",
    )(place, matrix, select)


def extra_kernel(place_ref, select_ref, own_ref, other_ref, out_ref, flat_ref):
    total = None
    for part, lower_ref in enumerate((own_ref, other_ref)):
        lower = lower_ref[...]
        high, rest = split_two(lower)
        middle, low = split_two(lower - high.astype(F32))
        select = select_ref[part]
        for piece in (high, middle, low):
            rows = jnp.dot(select, piece, preferred_element_type=F32)
            total = rows if total is None else total + rows
    flat_ref[: 2 * NB] = total[:, :LANES]
    flat_ref[2 * NB :] = total[:, LANES:]
    for one in range(4):
        for two in range(4):
            share = chip_at(place_ref, one, two) * 2 + place_ref[0]
            start = pl.multiple_of(share * EXTRA, EXTRA)
            out_ref[one, two] = flat_ref[pl.ds(start, EXTRA)]


def pick_extra(place, select, own, other):
    return pl.pallas_call(
        extra_kernel,
        out_shape=jax.ShapeDtypeStruct((4, 4, EXTRA, LANES), F32),
        in_specs=[pl.BlockSpec(memory_space=pltpu.SMEM)]
        + [pl.BlockSpec(memory_space=pltpu.VMEM)] * 3,
        scratch_shapes=[pltpu.VMEM((4 * NB, LANES), F32)],
        compiler_params=pltpu.CompilerParams(vmem_limit_bytes=16 << 20),
        cost_estimate=pl.CostEstimate(
            flops=2 * 3 * 512 * 1536 * 256, bytes_accessed=4 << 20, transcendentals=0
        ),
        name="pick_extra",
    )(place, select, own, other)


def solve_kernel(raw_ref, inverse_ref, out_ref):
    out_ref[:NB] = exact_dot(inverse_ref[0], raw_ref[:NB])
    out_ref[NB : 2 * NB] = exact_dot(inverse_ref[1], raw_ref[NB : 2 * NB])
    out_ref[2 * NB :] = raw_ref[2 * NB :]


def solve(raw, inverses):
    return pl.pallas_call(
        solve_kernel,
        out_shape=jax.ShapeDtypeStruct((SHARE, LANES), F32),
        cost_estimate=pl.CostEstimate(
            flops=6 * 2 * 2 * 256 * 256 * 128, bytes_accessed=1 << 20, transcendentals=0
        ),
        name="solve",
    )(raw, inverses)


def tops_kernel(
    place_ref, matrix_ref, top_ref, other_ref, take_ref, out_ref, left_ref, tops_ref, blocks_ref,
    in_sems, out_sems,
):
    width = 2 * LANES

    def lanes(step):
        return pl.ds(pl.multiple_of(step * width, width), width)

    def fetches(step):
        core = place_ref[0]
        return (
            pltpu.make_async_copy(
                top_ref.at[:, lanes(step)], tops_ref.at[step, core], in_sems.at[0, step]
            ),
            pltpu.make_async_copy(
                other_ref.at[:, lanes(step)], tops_ref.at[step, 1 - core], in_sems.at[1, step]
            ),
            pltpu.make_async_copy(
                matrix_ref.at[:, lanes(step)], blocks_ref.at[step], in_sems.at[2, step]
            ),
        )

    def store(step):
        return pltpu.make_async_copy(
            blocks_ref.at[step], out_ref.at[:, lanes(step)], out_sems.at[step]
        )

    @pl.loop(0, 16)
    def _(step):
        for copy in fetches(step):
            copy.start()

    left_ref[:, : 2 * NB] = take_ref[...]
    left_ref[:, 2 * NB :] = take_ref[...]

    @pl.loop(0, 16)
    def _(step):
        for copy in fetches(step):
            copy.wait()
        high, low = split_two(jnp.concatenate([tops_ref[step, 0], tops_ref[step, 1]], axis=0))
        right = jnp.concatenate([high, low], axis=0)
        total = jnp.dot(left_ref[...], right, preferred_element_type=F32)
        blocks_ref[step] = blocks_ref[step] + total
        store(step).start()

    @pl.loop(0, 16)
    def _(step):
        store(step).wait()


def put_tops(place, matrix, tops, other_tops, take):
    rows = matrix.shape[0]
    hbm = pl.BlockSpec(memory_space=pl.ANY)
    vmem = pl.BlockSpec(memory_space=pltpu.VMEM)
    return pl.pallas_call(
        tops_kernel,
        out_shape=jax.ShapeDtypeStruct(matrix.shape, F32),
        in_specs=[pl.BlockSpec(memory_space=pltpu.SMEM), hbm, hbm, hbm, vmem],
        out_specs=hbm,
        input_output_aliases={1: 0},
        scratch_shapes=[
            pltpu.VMEM((rows, 4 * NB), BF16),
            pltpu.VMEM((16, 2, NB, 2 * LANES), F32),
            pltpu.VMEM((16, rows, 2 * LANES), F32),
            pltpu.SemaphoreType.DMA((3, 16)),
            pltpu.SemaphoreType.DMA((16,)),
        ],
        compiler_params=pltpu.CompilerParams(vmem_limit_bytes=52 << 20),
        cost_estimate=pl.CostEstimate(
            flops=2 * rows * 4096 * 4 * NB, bytes_accessed=32 << 20, transcendentals=0
        ),
        name="put_tops",
    )(place, matrix, tops, other_tops, take)


def update_kernel(
    place_ref, source_ref, keep_ref, hit_ref, lower0_ref, lower1_ref, inverse_ref, *refs
):
    pieces = refs[:16]
    out_ref, left_ref, held_ref, flat_ref, blocks_ref, piece_sems, in_sems, out_sems = refs[16:]
    core, rank = place_ref[0], place_ref[3]
    width = 2 * LANES

    def copies_of(first, count, part):
        return [
            pltpu.make_async_copy(
                pieces[side * 8 + slot].at[:, pl.ds(first, count)],
                held_ref.at[side, slot // 2, pl.ds(slot % 2 * 2, 2), pl.ds(first, count)],
                piece_sems.at[part, side * 8 + slot],
            )
            for side in range(2)
            for slot in range(8)
        ]

    def in_order(lower_ref):
        piece = lower_ref.shape[0] // 4
        starts = [(i + 4 - place_ref[4]) % 4 * piece for i in range(4)]
        return jnp.concatenate([lower_ref[pl.ds(pl.multiple_of(i, 8), piece)] for i in starts])

    extras, copies = copies_of(2 * NB, EXTRA, 0), copies_of(0, 2 * NB, 1)
    for copy in extras + copies:
        copy.start()

    def lanes(step):
        chip = chip_at(place_ref, step // 4, step % 4)
        return pl.ds(pl.multiple_of(chip * width, width), width)

    def fetch(step):
        return pltpu.make_async_copy(
            source_ref.at[:, lanes(step)], blocks_ref.at[step], in_sems.at[step]
        )

    def store(step):
        return pltpu.make_async_copy(
            blocks_ref.at[step], out_ref.at[:, lanes(step)], out_sems.at[step]
        )

    @pl.loop(0, 16)
    def _(step):
        fetch(step).start()

    for copy in extras:
        copy.wait()
    for side in range(2):
        for turn in range(4):
            for inner in range(4):
                one, two = (turn, inner) if side == 0 else (inner, turn)
                owner = chip_at(place_ref, one, two) * 2 + (core + side) % 2
                start = pl.multiple_of(owner * EXTRA, EXTRA)
                flat_ref[pl.ds(start, EXTRA)] = held_ref[side, turn, inner, 2 * NB :]
    pivot_rows = jnp.concatenate([flat_ref[:NB], flat_ref[2 * NB : 3 * NB]], axis=1)
    top_rows = jnp.concatenate([flat_ref[NB : 2 * NB], flat_ref[3 * NB :]], axis=1)
    weight = exact_dot(inverse_ref[1], pivot_rows)
    hit = hit_ref[...].astype(F32)
    swapped = jnp.max(hit, axis=1, keepdims=True) > 0.0
    lower0 = jnp.where(swapped, exact_dot(hit, top_rows), in_order(lower0_ref))
    lower1 = in_order(lower1_ref)
    lower0 = lower0 - exact_dot(lower1, weight)
    at_second = rank == 1
    lower0 = jnp.concatenate([jnp.where(at_second, weight, lower0[:NB]), lower0[NB:]], axis=0)
    lower1 = jnp.concatenate([jnp.where(at_second, 0.0, lower1[:NB]), lower1[NB:]], axis=0)
    high, low = split_two(-jnp.concatenate([lower0, lower1], axis=1))
    for i, part in enumerate((high, high, low)):
        left_ref[:, i * 2 * NB : (i + 1) * 2 * NB] = part
    for copy in copies:
        copy.wait()

    @pl.loop(0, 16)
    def _(step):
        own = held_ref[0, step // 4, step % 4, : 2 * NB]
        other = held_ref[1, step % 4, step // 4, : 2 * NB]
        upper = jnp.concatenate(
            [jnp.where(core == 0, own, other), jnp.where(core == 0, other, own)], axis=1
        )
        fetch(step).wait()
        high, low = split_two(upper)
        right = jnp.concatenate([high, low, high], axis=0)
        total = jnp.dot(left_ref[...], right, preferred_element_type=F32)
        total = blocks_ref[step] * keep_ref[...] + total
        start = jnp.where(at_second, total[:NB] + upper[NB:], total[:NB])
        blocks_ref[step, :NB] = jnp.where(rank == 0, upper[:NB], start)
        blocks_ref[step, NB:] = total[NB:]
        store(step).start()

    @pl.loop(0, 16)
    def _(step):
        store(step).wait()


def update(place, source, keep, hit, lower0, lower1, inverse, pieces):
    rows, columns = source.shape
    hbm = pl.BlockSpec(memory_space=pl.ANY)
    vmem = pl.BlockSpec(memory_space=pltpu.VMEM)
    return pl.pallas_call(
        update_kernel,
        out_shape=jax.ShapeDtypeStruct(source.shape, F32),
        in_specs=[pl.BlockSpec(memory_space=pltpu.SMEM), hbm] + [vmem] * 5 + [hbm] * 16,
        out_specs=hbm,
        scratch_shapes=[
            pltpu.VMEM((rows, 6 * NB), BF16),
            pltpu.VMEM((2, 4, 4, SHARE, LANES), F32),
            pltpu.VMEM((4 * NB, LANES), F32),
            pltpu.VMEM((16, rows, 2 * LANES), F32),
            pltpu.SemaphoreType.DMA((2, 16)),
            pltpu.SemaphoreType.DMA((16,)),
            pltpu.SemaphoreType.DMA((16,)),
        ],
        compiler_params=pltpu.CompilerParams(vmem_limit_bytes=52 << 20),
        cost_estimate=pl.CostEstimate(
            flops=2 * rows * columns * 6 * NB, bytes_accessed=33 << 20, transcendentals=0
        ),
        name="update",
    )(place, source, keep, hit, lower0, lower1, inverse, *pieces)


def own_tops_kernel(place_ref, matrix_ref, out_ref, held_ref, sems):
    at_root = place_ref[3] < 2
    part = NB // 4
    chunks = [pl.ds(i * part, part) for i in range(4)]
    loads = [
        pltpu.make_async_copy(matrix_ref.at[rows], held_ref.at[rows], sems.at[0, i])
        for i, rows in enumerate(chunks)
    ]
    stores = [
        pltpu.make_async_copy(held_ref.at[rows], out_ref.at[rows], sems.at[1, i])
        for i, rows in enumerate(chunks)
    ]

    @pl.when(at_root)
    def _():
        for load in loads:
            load.start()
        for load, store in zip(loads, stores):
            load.wait()
            store.start()

    @pl.when(jnp.logical_not(at_root))
    def _():
        held_ref[...] = jnp.zeros_like(held_ref)
        for store in stores:
            store.start()

    for store in stores:
        store.wait()


def own_tops(place, matrix):
    columns = matrix.shape[1]
    hbm = pl.BlockSpec(memory_space=pl.ANY)
    return pl.pallas_call(
        own_tops_kernel,
        out_shape=jax.ShapeDtypeStruct((NB, columns), F32),
        in_specs=[pl.BlockSpec(memory_space=pltpu.SMEM), hbm],
        out_specs=hbm,
        scratch_shapes=[pltpu.VMEM((NB, columns), F32), pltpu.SemaphoreType.DMA((2, 4))],
        compiler_params=pltpu.CompilerParams(vmem_limit_bytes=VMEM_LIMIT),
        cost_estimate=pl.CostEstimate(flops=0, bytes_accessed=4 << 20, transcendentals=0),
        name="own_tops",
    )(place, matrix)


def body(matrix, lower_panels, inverses, pivots):
    rank = lax.axis_index("prow")
    column_rank = lax.axis_index("pcol")
    y, z, core = rank // 8, rank // 2 % 4, rank % 2
    first = jnp.where(core == 0, z, y)
    second = jnp.where(core == 0, y, z)
    rows = matrix.shape[0]
    index = jnp.arange(NB, dtype=jnp.int32)
    place = jnp.stack([core, y, z, rank, column_rank]).astype(jnp.int32)
    other_place = jnp.stack([1 - core, y, z, rank]).astype(jnp.int32)

    same_core = [[rank_of(y, z, core) for y in range(4) for z in range(4)] for core in range(2)]
    tops = lax.psum(own_tops(place, matrix), "prow", axis_index_groups=same_core)

    pairs = [[(i, (i - d) % 4) for i in range(4)] for d in (1, 2, 3)]
    lower = [lower_panels] + [lax.ppermute(lower_panels, "pcol", pair) for pair in pairs]
    lower_own, lower_last = (jnp.concatenate([part[panel] for part in lower]) for panel in range(2))


    pivot0, pivot1 = pivots[0], pivots[1]
    again = pivot1[:, None] == pivot0[None, :]
    from_top = jnp.any(again, axis=1)
    source1 = jnp.where(from_top, jnp.sum(jnp.where(again, index[None, :], 0), axis=1), pivot1)
    sources = jnp.concatenate([pivot0, source1])

    def local(matrix_row, owner=rank):
        blocks = matrix_row // NB
        where = blocks // 32 * NB + matrix_row % NB
        return jnp.where(blocks % 32 == owner, where, -1)

    local_row = jnp.arange(rows, dtype=jnp.int32)
    select = (local(sources)[:, None] == local_row[None, :]).astype(BF16)

    panel_rows = jnp.concatenate([pivot1, NB + index])
    want = jnp.stack([local(panel_rows), local(panel_rows, rank ^ 1)])
    piece = lower_panels.shape[1]
    away = (want // piece - column_rank) % 4 * piece + want % piece
    want = jnp.where(want >= 0, away, -1)
    want = (want[:, :, None] == local_row[None, None, :]).astype(BF16)

    lower_other = swap_cores(lower_own)
    sent = pick_rows(other_place, select, matrix)
    own_place, sent = lax.optimization_barrier((place, sent))
    other = swap_cores(sent)

    kept = pick_rows(own_place, select, matrix)

    def exchange():
        extra = pick_extra(place, want, lower_own, lower_other)
        part = [jnp.concatenate([kept[d] + other[d], extra[d]], axis=1) for d in range(4)]
        ahead = send(part[2][:2], one=1)
        behind = send(part[2][2:], one=3)
        high = part[0][2:] + send(part[1][2:], one=1)
        low = part[0][:2] + send(part[3][:2], one=3)
        low = low + send(part[1][:2] + ahead, one=1)
        high = high + send(part[3][2:] + behind, one=3)
        raw = low[0] + send(high[0], two=2) + send(low[1], two=1) + send(high[1], two=3)

        share = solve(raw, inverses)

        near = {d: send(share, two=4 - d) for d in (1, 2, 3)}
        low = jnp.stack([share, near[1]])
        high = jnp.stack([near[2], near[3]])

        late, high = lax.optimization_barrier((pivots, high))
        pivot0, pivot1 = late[0], late[1]
        again = pivot1[:, None] == pivot0[None, :]
        takes0 = (pivot0 >= 2 * NB) & ~jnp.any(again, axis=0)
        place0 = jnp.where(takes0, local(pivot0), -1)
        hit0 = local_row[:, None] == place0[None, :]
        hit1 = local_row[:, None] == local(pivot1)[None, :]
        shifted = (NB + index)[:, None] == pivot0[None, :]
        top1 = jnp.where(
            jnp.any(shifted, axis=1),
            jnp.sum(jnp.where(shifted, index[None, :], 0), axis=1),
            NB + index,
        )
        to_top = (top1[:, None] == jnp.arange(2 * NB, dtype=jnp.int32)[None, :]).astype(BF16)
        hit1 = hit1.astype(BF16)
        take = jnp.dot(hit1, to_top, preferred_element_type=F32)
        take = take + jnp.concatenate([hit0, jnp.zeros_like(hit0)], axis=1).astype(F32)
        replaced = jnp.any(hit1 > 0, axis=1) | jnp.any(hit0, axis=1)
        replaced = replaced | ((rank == 1) & (local_row < NB))
        keep = jnp.where(replaced, 0.0, 1.0).astype(F32)[:, None]
        take = take.astype(BF16)


        low_before, high_after = send(low, one=1), send(high, one=3)
        high_before, low_after = send(high, one=1), send(low, one=3)
        low_across, high_across = send(low_before, one=1), send(high_after, one=3)
        pieces = [
            low, high, low_after, high_after, low_across, high_across, low_before, high_before
        ]
        pieces = pieces + [swap_cores(value) for value in pieces]
        return pieces, keep, take, hit1

    def blank():
        return jax.tree.map(lambda leaf: jnp.zeros(leaf.shape, leaf.dtype), jax.eval_shape(exchange))

    pieces, keep, take, hit1 = lax.cond(pivots[0, 0] >= 0, exchange, blank)
    tops, pieces[0] = lax.optimization_barrier((tops, pieces[0]))
    other_tops = swap_cores(tops)
    result = update(place, matrix, keep, hit1, lower_own, lower_last, inverses, pieces)
    return put_tops(place, result, tops, other_tops, take)


def solution(mesh):
    placed = (P("prow", "pcol"), P(None, ("prow", "pcol"), None), P(), P())
    return jax.shard_map(
        body, mesh=mesh, in_specs=placed, out_specs=P("prow", "pcol"), check_vma=False
    )
```

```python
import jax
import jax.numpy as jnp
from jax import lax
from jax.experimental import pallas as pl
from jax.experimental.pallas import tpu as pltpu
from jax.sharding import PartitionSpec as P

F32 = jnp.float32
BF16 = jnp.bfloat16
HIGHEST = lax.Precision.HIGHEST
NB = 256
LANES = 128
EXTRA = 32
SHARE = 2 * NB + EXTRA
VMEM_LIMIT = 56 * 1024 * 1024


def rank_of(y, z, core):
    return ((y % 4) * 4 + z % 4) * 2 + core


def moved(y, z, core, one, two):
    return (y + two, z + one, core) if core == 0 else (y + one, z + two, core)


def send(value, one=0, two=0, only=lambda one, two: True):
    pairs = []
    for y in range(4):
        for z in range(4):
            for core in range(2):
                at = (z, y) if core == 0 else (y, z)
                if only(*at):
                    pairs.append((rank_of(y, z, core), rank_of(*moved(y, z, core, one, two))))
    return lax.ppermute(value, "prow", pairs)


def swap_cores(value):
    return lax.ppermute(value, "prow", [(rank, rank ^ 1) for rank in range(32)])


def split_two(value):
    high = value.astype(BF16)
    low = (value - high.astype(F32)).astype(BF16)
    return high, low


def exact_dot(a, b):
    return jnp.dot(a, b, precision=HIGHEST, preferred_element_type=F32)


def chip_at(place, one, two):
    by_z = (place[1] + two) % 4 * 4 + (place[2] + one) % 4
    by_y = (place[1] + one) % 4 * 4 + (place[2] + two) % 4
    return jnp.where(place[0] == 0, by_z, by_y)


def pick_kernel(place_ref, matrix_ref, select_ref, out_ref, left_ref, blocks_ref, rows_ref, in_sems, out_sems):
    def fetches(one):
        return [
            pltpu.make_async_copy(
                matrix_ref.at[:, pl.ds(pl.multiple_of(share * LANES, LANES), LANES)],
                blocks_ref.at[one, :, pl.ds(two * LANES, LANES)],
                in_sems.at[one, two],
            )
            for two in range(4)
            for share in [chip_at(place_ref, one, two) * 2 + place_ref[0]]
        ]

    def store(one):
        return pltpu.make_async_copy(rows_ref.at[one], out_ref.at[one], out_sems.at[one])

    for one in range(4):
        for copy in fetches(one):
            copy.start()
    for part in range(2):
        left_ref[:, part * select_ref.shape[1] : (part + 1) * select_ref.shape[1]] = select_ref[...]

    @pl.loop(0, 4)
    def _(one):
        for copy in fetches(one):
            copy.wait()
        right = jnp.concatenate(split_two(blocks_ref[one]), axis=0)
        rows = jnp.dot(left_ref[...], right, preferred_element_type=F32)
        for two in range(4):
            rows_ref[one, two] = rows[:, two * LANES : (two + 1) * LANES]
        store(one).start()

    for one in range(4):
        store(one).wait()


def pick_rows(place, select, matrix):
    rows = matrix.shape[0]
    hbm = pl.BlockSpec(memory_space=pl.ANY)
    shape = (4, 4, 2 * NB, LANES)
    return pl.pallas_call(
        pick_kernel,
        out_shape=jax.ShapeDtypeStruct(shape, F32),
        in_specs=[
            pl.BlockSpec(memory_space=pltpu.SMEM), hbm, pl.BlockSpec(memory_space=pltpu.VMEM)
        ],
        out_specs=hbm,
        scratch_shapes=[
            pltpu.VMEM((2 * NB, 2 * rows), BF16),
            pltpu.VMEM((4, rows, 4 * LANES), F32),
            pltpu.VMEM(shape, F32),
            pltpu.SemaphoreType.DMA((4, 4)),
            pltpu.SemaphoreType.DMA((4,)),
        ],
        compiler_params=pltpu.CompilerParams(vmem_limit_bytes=52 << 20),
        cost_estimate=pl.CostEstimate(
            flops=2 * 2 * 512 * 768 * 2048, bytes_accessed=10 << 20, transcendentals=0
        ),
        name="pick_rows",
    )(place, matrix, select)


def extra_kernel(place_ref, select_ref, own_ref, other_ref, out_ref, flat_ref):
    total = None
    for part, lower_ref in enumerate((own_ref, other_ref)):
        lower = lower_ref[...]
        high, rest = split_two(lower)
        middle, low = split_two(lower - high.astype(F32))
        select = select_ref[part]
        for piece in (high, middle, low):
            rows = jnp.dot(select, piece, preferred_element_type=F32)
            total = rows if total is None else total + rows
    flat_ref[: 2 * NB] = total[:, :LANES]
    flat_ref[2 * NB :] = total[:, LANES:]
    for one in range(4):
        for two in range(4):
            share = chip_at(place_ref, one, two) * 2 + place_ref[0]
            start = pl.multiple_of(share * EXTRA, EXTRA)
            out_ref[one, two] = flat_ref[pl.ds(start, EXTRA)]


def pick_extra(place, select, own, other):
    return pl.pallas_call(
        extra_kernel,
        out_shape=jax.ShapeDtypeStruct((4, 4, EXTRA, LANES), F32),
        in_specs=[pl.BlockSpec(memory_space=pltpu.SMEM)]
        + [pl.BlockSpec(memory_space=pltpu.VMEM)] * 3,
        scratch_shapes=[pltpu.VMEM((4 * NB, LANES), F32)],
        compiler_params=pltpu.CompilerParams(vmem_limit_bytes=16 << 20),
        cost_estimate=pl.CostEstimate(
            flops=2 * 3 * 512 * 1536 * 256, bytes_accessed=4 << 20, transcendentals=0
        ),
        name="pick_extra",
    )(place, select, own, other)


def solve_kernel(raw_ref, inverse_ref, out_ref):
    out_ref[:NB] = exact_dot(inverse_ref[0], raw_ref[:NB])
    out_ref[NB : 2 * NB] = exact_dot(inverse_ref[1], raw_ref[NB : 2 * NB])
    out_ref[2 * NB :] = raw_ref[2 * NB :]


def solve(raw, inverses):
    return pl.pallas_call(
        solve_kernel,
        out_shape=jax.ShapeDtypeStruct((SHARE, LANES), F32),
        cost_estimate=pl.CostEstimate(
            flops=6 * 2 * 2 * 256 * 256 * 128, bytes_accessed=1 << 20, transcendentals=0
        ),
        name="solve",
    )(raw, inverses)


def tops_kernel(
    matrix_ref, top_ref, take_ref, out_ref, left_ref, tops_ref, blocks_ref, in_sems, out_sems
):
    width = 2 * LANES

    def lanes(step):
        return pl.ds(pl.multiple_of(step * width, width), width)

    def fetches(step):
        return (
            pltpu.make_async_copy(top_ref.at[:, lanes(step)], tops_ref.at[step], in_sems.at[0, step]),
            pltpu.make_async_copy(
                matrix_ref.at[:, lanes(step)], blocks_ref.at[step], in_sems.at[1, step]
            ),
        )

    def store(step):
        return pltpu.make_async_copy(
            blocks_ref.at[step], out_ref.at[:, lanes(step)], out_sems.at[step]
        )

    @pl.loop(0, 16)
    def _(step):
        for copy in fetches(step):
            copy.start()

    left_ref[:, : 2 * NB] = take_ref[...]
    left_ref[:, 2 * NB :] = take_ref[...]

    @pl.loop(0, 16)
    def _(step):
        for copy in fetches(step):
            copy.wait()
        high, low = split_two(tops_ref[step])
        right = jnp.concatenate([high, low], axis=0)
        total = jnp.dot(left_ref[...], right, preferred_element_type=F32)
        blocks_ref[step] = blocks_ref[step] + total
        store(step).start()

    @pl.loop(0, 16)
    def _(step):
        store(step).wait()


def put_tops(matrix, tops, take):
    rows = matrix.shape[0]
    hbm = pl.BlockSpec(memory_space=pl.ANY)
    vmem = pl.BlockSpec(memory_space=pltpu.VMEM)
    return pl.pallas_call(
        tops_kernel,
        out_shape=jax.ShapeDtypeStruct(matrix.shape, F32),
        in_specs=[hbm, hbm, vmem],
        out_specs=hbm,
        input_output_aliases={0: 0},
        scratch_shapes=[
            pltpu.VMEM((rows, 4 * NB), BF16),
            pltpu.VMEM((16, 2 * NB, 2 * LANES), F32),
            pltpu.VMEM((16, rows, 2 * LANES), F32),
            pltpu.SemaphoreType.DMA((2, 16)),
            pltpu.SemaphoreType.DMA((16,)),
        ],
        compiler_params=pltpu.CompilerParams(vmem_limit_bytes=52 << 20),
        cost_estimate=pl.CostEstimate(
            flops=2 * rows * 4096 * 4 * NB, bytes_accessed=32 << 20, transcendentals=0
        ),
        name="put_tops",
    )(matrix, tops, take)


def update_kernel(place_ref, source_ref, keep_ref, hit_ref, lower_ref, inverse_ref, *refs):
    pieces = refs[:16]
    out_ref, left_ref, held_ref, flat_ref, blocks_ref, piece_sems, in_sems, out_sems = refs[16:]
    core, rank = place_ref[0], place_ref[3]
    width = 2 * LANES

    def copies_of(first, count, part):
        return [
            pltpu.make_async_copy(
                pieces[side * 8 + slot].at[:, pl.ds(first, count)],
                held_ref.at[side, slot // 2, pl.ds(slot % 2 * 2, 2), pl.ds(first, count)],
                piece_sems.at[part, side * 8 + slot],
            )
            for side in range(2)
            for slot in range(8)
        ]

    extras, copies = copies_of(2 * NB, EXTRA, 0), copies_of(0, 2 * NB, 1)
    for copy in extras + copies:
        copy.start()

    def lanes(step):
        chip = chip_at(place_ref, step // 4, step % 4)
        return pl.ds(pl.multiple_of(chip * width, width), width)

    def fetch(step):
        return pltpu.make_async_copy(
            source_ref.at[:, lanes(step)], blocks_ref.at[step], in_sems.at[step]
        )

    def store(step):
        return pltpu.make_async_copy(
            blocks_ref.at[step], out_ref.at[:, lanes(step)], out_sems.at[step]
        )

    @pl.loop(0, 16)
    def _(step):
        fetch(step).start()

    for copy in extras:
        copy.wait()
    for side in range(2):
        for turn in range(4):
            for inner in range(4):
                one, two = (turn, inner) if side == 0 else (inner, turn)
                owner = chip_at(place_ref, one, two) * 2 + (core + side) % 2
                start = pl.multiple_of(owner * EXTRA, EXTRA)
                flat_ref[pl.ds(start, EXTRA)] = held_ref[side, turn, inner, 2 * NB :]
    pivot_rows = jnp.concatenate([flat_ref[:NB], flat_ref[2 * NB : 3 * NB]], axis=1)
    top_rows = jnp.concatenate([flat_ref[NB : 2 * NB], flat_ref[3 * NB :]], axis=1)
    weight = exact_dot(inverse_ref[1], pivot_rows)
    hit = hit_ref[...].astype(F32)
    swapped = jnp.max(hit, axis=1, keepdims=True) > 0.0
    lower0 = jnp.where(swapped, exact_dot(hit, top_rows), lower_ref[0])
    lower1 = lower_ref[1]
    lower0 = lower0 - exact_dot(lower1, weight)
    at_second = rank == 1
    lower0 = jnp.concatenate([jnp.where(at_second, weight, lower0[:NB]), lower0[NB:]], axis=0)
    lower1 = jnp.concatenate([jnp.where(at_second, 0.0, lower1[:NB]), lower1[NB:]], axis=0)
    high, low = split_two(-jnp.concatenate([lower0, lower1], axis=1))
    for i, part in enumerate((high, high, low)):
        left_ref[:, i * 2 * NB : (i + 1) * 2 * NB] = part
    for copy in copies:
        copy.wait()

    @pl.loop(0, 16)
    def _(step):
        own = held_ref[0, step // 4, step % 4, : 2 * NB]
        other = held_ref[1, step % 4, step // 4, : 2 * NB]
        upper = jnp.concatenate(
            [jnp.where(core == 0, own, other), jnp.where(core == 0, other, own)], axis=1
        )
        fetch(step).wait()
        high, low = split_two(upper)
        right = jnp.concatenate([high, low, high], axis=0)
        total = jnp.dot(left_ref[...], right, preferred_element_type=F32)
        total = blocks_ref[step] * keep_ref[...] + total
        start = jnp.where(at_second, total[:NB] + upper[NB:], total[:NB])
        blocks_ref[step, :NB] = jnp.where(rank == 0, upper[:NB], start)
        blocks_ref[step, NB:] = total[NB:]
        store(step).start()

    @pl.loop(0, 16)
    def _(step):
        store(step).wait()


def update(place, source, keep, hit, lower, inverse, pieces):
    rows, columns = source.shape
    hbm = pl.BlockSpec(memory_space=pl.ANY)
    vmem = pl.BlockSpec(memory_space=pltpu.VMEM)
    return pl.pallas_call(
        update_kernel,
        out_shape=jax.ShapeDtypeStruct(source.shape, F32),
        in_specs=[pl.BlockSpec(memory_space=pltpu.SMEM), hbm] + [vmem] * 4 + [hbm] * 16,
        out_specs=hbm,
        scratch_shapes=[
            pltpu.VMEM((rows, 6 * NB), BF16),
            pltpu.VMEM((2, 4, 4, SHARE, LANES), F32),
            pltpu.VMEM((4 * NB, LANES), F32),
            pltpu.VMEM((16, rows, 2 * LANES), F32),
            pltpu.SemaphoreType.DMA((2, 16)),
            pltpu.SemaphoreType.DMA((16,)),
            pltpu.SemaphoreType.DMA((16,)),
        ],
        compiler_params=pltpu.CompilerParams(vmem_limit_bytes=52 << 20),
        cost_estimate=pl.CostEstimate(
            flops=2 * rows * columns * 6 * NB, bytes_accessed=33 << 20, transcendentals=0
        ),
        name="update",
    )(place, source, keep, hit, lower, inverse, *pieces)


def own_tops_kernel(place_ref, matrix_ref, out_ref, zero_ref, held_ref, sems, zero_sems):
    rank = place_ref[3]
    zero_ref[...] = jnp.zeros_like(zero_ref)
    width = zero_ref.shape[1]

    def blanks(panel):
        return [
            pltpu.make_async_copy(
                zero_ref,
                out_ref.at[pl.ds(panel * NB, NB), pl.ds(i * width, width)],
                zero_sems.at[panel, i],
            )
            for i in range(4)
        ]

    for panel in range(2):

        @pl.when(rank != panel)
        def _(panel=panel):
            for copy in blanks(panel):
                copy.start()

    for panel in range(2):

        @pl.when(rank == panel)
        def _(panel=panel):
            part = NB // 4
            chunks = [pl.ds(i * part, part) for i in range(4)]
            loads = [
                pltpu.make_async_copy(matrix_ref.at[rows], held_ref.at[rows], sems.at[0, i])
                for i, rows in enumerate(chunks)
            ]
            stores = [
                pltpu.make_async_copy(
                    held_ref.at[rows], out_ref.at[pl.ds(panel * NB + i * part, part)], sems.at[1, i]
                )
                for i, rows in enumerate(chunks)
            ]
            for load in loads:
                load.start()
            for load, store in zip(loads, stores):
                load.wait()
                store.start()
            for store in stores:
                store.wait()

    for panel in range(2):

        @pl.when(rank != panel)
        def _(panel=panel):
            for copy in blanks(panel):
                copy.wait()


def own_tops(place, matrix):
    columns = matrix.shape[1]
    hbm = pl.BlockSpec(memory_space=pl.ANY)
    return pl.pallas_call(
        own_tops_kernel,
        out_shape=jax.ShapeDtypeStruct((2 * NB, columns), F32),
        in_specs=[pl.BlockSpec(memory_space=pltpu.SMEM), hbm],
        out_specs=hbm,
        scratch_shapes=[
            pltpu.VMEM((NB, columns // 4), F32),
            pltpu.VMEM((NB, columns), F32),
            pltpu.SemaphoreType.DMA((2, 4)),
            pltpu.SemaphoreType.DMA((2, 4)),
        ],
        compiler_params=pltpu.CompilerParams(vmem_limit_bytes=VMEM_LIMIT),
        cost_estimate=pl.CostEstimate(flops=0, bytes_accessed=8 << 20, transcendentals=0),
        name="own_tops",
    )(place, matrix)


def body(matrix, lower_panels, inverses, pivots):
    rank = lax.axis_index("prow")
    column_rank = lax.axis_index("pcol")
    y, z, core = rank // 8, rank // 2 % 4, rank % 2
    first = jnp.where(core == 0, z, y)
    second = jnp.where(core == 0, y, z)
    rows = matrix.shape[0]
    index = jnp.arange(NB, dtype=jnp.int32)
    place = jnp.stack([core, y, z, rank]).astype(jnp.int32)
    other_place = jnp.stack([1 - core, y, z, rank]).astype(jnp.int32)

    tops = lax.psum(own_tops(place, matrix), "prow")

    lower = lax.all_gather(lower_panels, "pcol", axis=1, tiled=True)
    lower_own = lower_panels[0]
    far = [lax.ppermute(lower_own, "pcol", [(i, (i - d) % 4) for i in range(4)]) for d in (1, 2, 3)]
    lower_own = jnp.concatenate([lower_own] + far)


    pivot0, pivot1 = pivots[0], pivots[1]
    again = pivot1[:, None] == pivot0[None, :]
    from_top = jnp.any(again, axis=1)
    source1 = jnp.where(from_top, jnp.sum(jnp.where(again, index[None, :], 0), axis=1), pivot1)
    sources = jnp.concatenate([pivot0, source1])

    def local(matrix_row, owner=rank):
        blocks = matrix_row // NB
        where = blocks // 32 * NB + matrix_row % NB
        return jnp.where(blocks % 32 == owner, where, -1)

    local_row = jnp.arange(rows, dtype=jnp.int32)
    select = (local(sources)[:, None] == local_row[None, :]).astype(BF16)

    panel_rows = jnp.concatenate([pivot1, NB + index])
    want = jnp.stack([local(panel_rows), local(panel_rows, rank ^ 1)])
    piece = lower_panels.shape[1]
    away = (want // piece - column_rank) % 4 * piece + want % piece
    want = jnp.where(want >= 0, away, -1)
    want = (want[:, :, None] == local_row[None, None, :]).astype(BF16)

    def exchange(turn, share):
        lower_other = swap_cores(jnp.where(turn == 0, lower_own, 0.0))
        sent = pick_rows(other_place + turn, select, matrix)
        own_place, sent = lax.optimization_barrier((place + turn, sent))
        other = swap_cores(sent)

        kept = pick_rows(own_place, select, matrix)
        extra = pick_extra(place, want, lower_own, lower_other)
        part = [jnp.concatenate([kept[d] + other[d], extra[d]], axis=1) for d in range(4)]
        ahead = send(part[2][:2], one=1)
        behind = send(part[2][2:], one=3)
        high = part[0][2:] + send(part[1][2:], one=1)
        low = part[0][:2] + send(part[3][:2], one=3)
        low = low + send(part[1][:2] + ahead, one=1)
        high = high + send(part[3][2:] + behind, one=3)
        raw = low[0] + send(high[0], two=2) + send(low[1], two=1) + send(high[1], two=3)

        return solve(raw, inverses)

    rounds = jnp.minimum(pivots[0, 0] + 1, 1)
    share = lax.fori_loop(0, rounds, exchange, jnp.zeros((SHARE, LANES), F32))

    near = {d: send(share, two=4 - d) for d in (1, 2, 3)}
    low = jnp.stack([share, near[1]])
    high = jnp.stack([near[2], near[3]])

    pivots, high = lax.optimization_barrier((pivots, high))
    pivot0, pivot1 = pivots[0], pivots[1]
    again = pivot1[:, None] == pivot0[None, :]
    takes0 = (pivot0 >= 2 * NB) & ~jnp.any(again, axis=0)
    place0 = jnp.where(takes0, local(pivot0), -1)
    hit0 = local_row[:, None] == place0[None, :]
    hit1 = local_row[:, None] == local(pivot1)[None, :]
    shifted = (NB + index)[:, None] == pivot0[None, :]
    top1 = jnp.where(
        jnp.any(shifted, axis=1),
        jnp.sum(jnp.where(shifted, index[None, :], 0), axis=1),
        NB + index,
    )
    to_top = (top1[:, None] == jnp.arange(2 * NB, dtype=jnp.int32)[None, :]).astype(BF16)
    hit1 = hit1.astype(BF16)
    take = jnp.dot(hit1, to_top, preferred_element_type=F32)
    take = take + jnp.concatenate([hit0, jnp.zeros_like(hit0)], axis=1).astype(F32)
    replaced = jnp.any(hit1 > 0, axis=1) | jnp.any(hit0, axis=1)
    replaced = replaced | ((rank == 1) & (local_row < NB))
    keep = jnp.where(replaced, 0.0, 1.0).astype(F32)[:, None]
    take = take.astype(BF16)


    low_before, high_after = send(low, one=1), send(high, one=3)
    high_before, low_after = send(high, one=1), send(low, one=3)
    low_across, high_across = send(low_before, one=1), send(high_after, one=3)
    pieces = [
        low, high, low_after, high_after, low_across, high_across, low_before, high_before
    ]
    pieces = pieces + [swap_cores(value) for value in pieces]
    result = update(place, matrix, keep, hit1, lower, inverses, pieces)
    return put_tops(result, tops, take)


def solution(mesh):
    placed = (P("prow", "pcol"), P(None, ("prow", "pcol"), None), P(), P())
    return jax.shard_map(
        body, mesh=mesh, in_specs=placed, out_specs=P("prow", "pcol"), check_vma=False
    )
```
